256 devices in a mesh: wide: 16 (over x_hi, z), narrow: 4 (over x_lo, core), seq: 4 (over y).
Axes of the slice: x: 4 (x_hi: 2, x_lo: 2; x = x_hi * 2 + x_lo), y: 4, z: 8, core: 2. Of those that a mesh axis runs over, the one named last changes fastest.
Arguments:
- attn_query: bfloat16 [8192, 73728], P(('seq', 'wide'), 'narrow'), parts along dimension 0, may hold values from -6 to 6
- key_latent: bfloat16 [8192, 576], P(('seq', 'wide')), parts along dimension 0, may hold values from -6 to 6
- lse_attn: float32 [128, 8192], P('narrow', ('seq', 'wide')), parts along dimension 1, may hold values from 1 to 3
- index_query: bfloat16 [8192, 8192], P(('seq', 'wide'), 'narrow'), parts along dimension 0, may hold values from -6 to 6
- index_key: bfloat16 [8192, 128], P(('seq', 'wide')), parts along dimension 0, may hold values from -6 to 6
- index_weight: float32 [64, 8192], P('narrow', ('seq', 'wide')), parts along dimension 1, may hold values from -0.75 to 0.75
- lse_index: float32 [8192], P(('seq', 'wide')), parts along dimension 0, may hold values from 0 to 1
- block_order: int32 [64], P('seq'), parts along dimension 0, may hold values from 0 to 1023, as said below
Outputs:
- d_index_query: float32 [8192, 8192], P(('seq', 'wide'), 'narrow'), parts along dimension 0
- d_index_weight: float32 [64, 8192], P('narrow', ('seq', 'wide')), parts along dimension 1
- d_index_key: float32 [8192, 128], P(('seq', 'wide')), parts along dimension 0
The draws below stay inside these ranges and needn't reach their ends.
There are 4 independent parts, one for each index of `seq`. The reference program is written for one: setup_inputs(seed, part) draws one part's arguments, and reference() takes and returns one part's arrays. A program takes and returns all parts, laid end to end along the dimension named above; each array names one. Nothing has to cross between parts.
Inputs may be any that keep to these rules, and one draw needn't show every extreme that they name: Index d of wide holds tokens 128 * block_order[d] to 128 * block_order[d] + 127 of the context; the values are distinct.
All inputs are finite; a program needn't handle non-finite values.
Results may differ from the reference program's by a relative error of at most 0.008.
Values may be sent and summed in bfloat16 or wider, within the bound.
A program may use at most 64 MiB of HBM per device.

```python
import jax
import jax.numpy as jnp
from jax import lax

HEADS = 128
KV_RANK = 512
ROPE = 64
IHEADS = 64
IDIM = 128
TOK_DEV = 128
KEY_WIDTH = 576
TOKENS = 2048
N_WIDE = 16


def draw_block_order(key, part):
    first_key, second_key = jax.random.split(jax.random.fold_in(key, 7331))
    span = 64 * N_WIDE
    chosen = jax.random.permutation(first_key, span - 1)[:N_WIDE - 1].astype(jnp.int32)
    values = jnp.concatenate([chosen, jnp.full((1,), span - 1, jnp.int32)])
    return jax.random.permutation(second_key, values).astype(jnp.int32)


def shard_levels(stream_key, shape, cuts, least, top_value):
    def one(axis_at, blocks):
        draws = jax.random.uniform(jax.random.fold_in(jax.random.fold_in(stream_key, 6), axis_at), (blocks,), jnp.float32, least / len(cuts), top_value / len(cuts))
        return jnp.repeat(jnp.exp(draws), shape[axis_at] // blocks).reshape((-1,) + (1,) * (len(shape) - axis_at - 1))

    loudness = one(*cuts[0])
    for cut in cuts[1:]:
        loudness = loudness * one(*cut)
    return loudness


def centred(key, extent, spread, most, pieces=(), held_as=jnp.bfloat16):
    drawn = jax.random.normal(key, extent, jnp.float32) * spread
    if len(pieces) > 0:
        drawn = shard_levels(key, extent, pieces, -0.22, 0.18) * drawn
    return jnp.clip(drawn, min=-most, max=most).astype(held_as)


def setup_inputs(seed: int = 0, part: int = 0) -> dict:
    seeds = jax.random.split(jax.random.key(seed), 9)
    part_keys = jax.random.split(jax.random.fold_in(seeds[8], part), 9)
    return {
        "attn_query": centred(part_keys[0], (TOKENS, HEADS * KEY_WIDTH), 1.0, 6.0, ((0, 16), (1, 4))),
        "key_latent": centred(part_keys[1], (TOKENS, KEY_WIDTH), 1.0, 6.0, ((0, 16),)),
        "lse_attn": jnp.clip(1.0 + 2.0 * jax.random.uniform(part_keys[2], (HEADS, TOKENS), jnp.float32) ** shard_levels(part_keys[2], (HEADS, TOKENS), ((0, 4), (1, 16)), -0.2, 0.2), 1.0, 3.0),
        "index_query": centred(part_keys[3], (TOKENS, IHEADS * IDIM), 1.0, 6.0, ((0, 16), (1, 4))),
        "index_key": centred(part_keys[4], (TOKENS, IDIM), 1.0, 6.0, ((0, 16),)),
        "index_weight": centred(part_keys[5], (IHEADS, TOKENS), IHEADS ** -0.5, 0.75, ((0, 4), (1, 16)), jnp.float32),
        "lse_index": jnp.clip(1.0 * jax.random.uniform(part_keys[6], (TOKENS,), jnp.float32) ** shard_levels(part_keys[6], (TOKENS,), ((0, 16),), -0.2, 0.2), 0.0, 1.0),
        "block_order": draw_block_order(jax.random.fold_in(jax.random.fold_in(seeds[8], part), 71), part),
    }


attn_scale = 192.0 ** -0.5


def reference(attn_query, key_latent, lse_attn, index_query, index_key, index_weight, lse_index, block_order):
    key_width = KV_RANK + ROPE
    query_heads = attn_query.reshape(TOKENS, HEADS, key_width)
    index_heads = index_query.reshape(TOKENS, IHEADS, IDIM)
    offsets = jnp.arange(TOKENS, dtype=jnp.int32)
    position = block_order[offsets // TOK_DEV].astype(jnp.int32) * TOK_DEV + offsets % TOK_DEV
    keys_full = key_latent.astype(jnp.float32)
    ikeys_full = index_key.astype(jnp.float32)
    index_scale = IDIM ** -0.5

    def one_block(key_total, block_index):
        start = (block_index * TOK_DEV).astype(jnp.int32)
        queries = lax.dynamic_slice_in_dim(query_heads, start, TOK_DEV, 0).astype(jnp.float32)
        iqueries = lax.dynamic_slice_in_dim(index_heads, start, TOK_DEV, 0).astype(jnp.float32)
        lse_rows = jnp.transpose(lax.dynamic_slice_in_dim(lse_attn, start, TOK_DEV, 1))
        weight_rows = jnp.transpose(lax.dynamic_slice_in_dim(index_weight, start, TOK_DEV, 1))
        lse_share = lax.dynamic_slice_in_dim(lse_index, start, TOK_DEV, 0)
        query_pos = lax.dynamic_slice_in_dim(position, start, TOK_DEV, 0)
        causal = query_pos[:, None] >= position[None, :]
        scores = jnp.einsum("thc,sc->ths", queries, keys_full) * attn_scale
        target = jnp.sum(jnp.exp(scores - lse_rows[:, :, None]), axis=1) / HEADS
        logits = jnp.einsum("tjc,sc->tjs", iqueries, ikeys_full) * index_scale
        active = jnp.maximum(logits, 0.0)
        score = jnp.einsum("tjs,tj->ts", active, weight_rows)
        difference = jnp.where(causal, jnp.exp(score - lse_share[:, None]) - target, 0.0)
        grad_weight = jnp.einsum("ts,tjs->jt", difference, active)
        coefficient = (difference[:, None, :] * weight_rows[:, :, None] * (logits > 0.0).astype(jnp.float32) * index_scale).astype(jnp.bfloat16)
        coef_full = coefficient.astype(jnp.float32)
        grad_query = jnp.einsum("tjs,sc->tjc", coef_full, ikeys_full)
        grad_key = jnp.einsum("tjs,tjc->sc", coef_full, iqueries)
        return key_total + grad_key, (grad_query, grad_weight)

    start_total = jnp.zeros((TOKENS, IDIM), jnp.float32)
    key_total, stacked = lax.scan(one_block, start_total, jnp.arange(N_WIDE, dtype=jnp.int32))
    grad_query, grad_weight = stacked
    d_index_query = grad_query.reshape(TOKENS, IHEADS * IDIM)
    d_index_weight = jnp.transpose(grad_weight, (1, 0, 2)).reshape(IHEADS, TOKENS)
    return d_index_query, d_index_weight, key_total
```

```python
import functools

import jax
import jax.numpy as jnp
from jax import lax
from jax.experimental import pallas as pl
from jax.experimental.pallas import tpu as pltpu
from jax.sharding import PartitionSpec as P

HEADS = 128
LOG2E = 1.4426950408889634
ATTN_SCALE2 = 192.0 ** (-0.5) * LOG2E
INDEX_SCALE = 128.0 ** (-0.5)
ROWS = 128
PAIR = 256
NT = (((1,), (1,)), ((), ()))
NN = (((1,), (0,)), ((), ()))
f32 = jnp.float32
bf16 = jnp.bfloat16


def twice(x):
    return jnp.concatenate([x, x], axis=1)


def prepare(lse_ref, weight_ref, lse_b, w_b):
    lse_t = jnp.transpose(lse_ref[...]) * LOG2E
    for h in range(32):
        lse_b[h] = jnp.broadcast_to(lse_t[:, h : h + 1], (ROWS, ROWS))
    w_t = jnp.transpose(weight_ref[...]) * INDEX_SCALE
    for j in range(16):
        w_b[j] = jnp.broadcast_to(w_t[:, j : j + 1], (ROWS, ROWS))


def target_sum(q_ref, kab, lse_b):
    group = 4
    total = None
    for g in range(16 // group):
        for par in range(2):
            parts = [
                q_ref[:, (g * group + i) * 1152 + par * 512 : (g * group + i) * 1152 + par * 512 + 640]
                for i in range(group)
            ]
            s = lax.dot_general(
                jnp.concatenate(parts, axis=0), kab[par], NT, preferred_element_type=f32
            )
            for i in range(group):
                h = (g * group + i) * 2 + par
                e = jnp.exp2(s[i * ROWS : (i + 1) * ROWS] * ATTN_SCALE2 - twice(lse_b[h]))
                total = e if total is None else total + e
    return total


def score_sum(iq_ref, ikey, w_b, keep):
    total = None
    for g in range(2):
        lhs = jnp.concatenate(
            [iq_ref[:, (g * 8 + i) * ROWS : (g * 8 + i + 1) * ROWS] for i in range(8)], axis=0
        )
        s = lax.dot_general(lhs, ikey, NT, preferred_element_type=f32)
        keep(g, s.astype(bf16))
        for i in range(8):
            e = jnp.maximum(s[i * ROWS : (i + 1) * ROWS], 0.0) * twice(w_b[g * 8 + i])
            total = e if total is None else total + e
    return total


def forward(q_ref, kx_ref, lse_ref, iq_ref, weight_ref, target_ref, score_ref, logit_ref, lse_b, w_b, kab):
    @pl.when(pl.program_id(0) == 0)
    def _():
        prepare(lse_ref, weight_ref, lse_b, w_b)

    kx = kx_ref[0]
    kab[0] = kx[:, 0:640]
    kab[1] = jnp.concatenate([kx[:, 576:640], kx[:, 0:576]], axis=1)
    target_ref[0] = target_sum(q_ref, kab, lse_b)

    def keep(g, x):
        logit_ref[0, g * 1024 : (g + 1) * 1024] = x

    score_ref[0] = score_sum(iq_ref, kx[:, 640:768], w_b, keep)


def backward(logit_ref, kx_ref, diff_ref, iq_ref, weight_ref, u_ref, dk_ref, wq):
    @pl.when(pl.program_id(0) == 0)
    def _():
        u_ref[...] = jnp.zeros_like(u_ref)
        for j in range(16):
            x = jnp.transpose(iq_ref[:, j * ROWS : (j + 1) * ROWS].astype(f32))
            x = x * (weight_ref[j : j + 1, :] * INDEX_SCALE)
            hi = x.astype(bf16)
            wq[0:128, j * ROWS : (j + 1) * ROWS] = hi
            wq[128:256, j * ROWS : (j + 1) * ROWS] = (x - hi.astype(f32)).astype(bf16)

    d = diff_ref[0]
    md = jnp.concatenate(
        [
            jnp.where(logit_ref[0, j * ROWS : (j + 1) * ROWS] > 0, d, jnp.zeros_like(d))
            for j in range(16)
        ],
        axis=0,
    )
    u_ref[...] += lax.dot_general(md, kx_ref[0, :, 640:768], NN, preferred_element_type=f32)
    both = lax.dot_general(wq[...], md, NN, preferred_element_type=f32)
    dk_ref[0] = both[0:128] + both[128:256]


def body(
    attn_query, key_latent, lse_attn, index_query, index_key, index_weight, lse_index, block_order
):
    place = lax.axis_index("wide")
    mine = jnp.concatenate(
        [key_latent, jnp.zeros((ROWS, 64), bf16), index_key], axis=1
    )
    kx = lax.all_gather(mine, "wide").reshape(8, PAIR, 768)
    sds = jax.ShapeDtypeStruct
    whole = lambda *shape: pl.BlockSpec(shape, lambda p: (0,) * len(shape))
    slab = lambda *shape: pl.BlockSpec((1,) + shape, lambda p: (p,) + (0,) * len(shape))
    params = pltpu.CompilerParams(vmem_limit_bytes=50 << 20)
    target, score, logit = pl.pallas_call(
        forward,
        grid=(8,),
        out_shape=(sds((8, ROWS, PAIR), f32), sds((8, ROWS, PAIR), f32), sds((8, 2048, PAIR), bf16)),
        in_specs=[whole(ROWS, 18432), slab(PAIR, 768), whole(32, ROWS), whole(ROWS, 2048), whole(16, ROWS)],
        out_specs=(slab(ROWS, PAIR), slab(ROWS, PAIR), slab(2048, PAIR)),
        scratch_shapes=[
            pltpu.VMEM((32, ROWS, ROWS), f32),
            pltpu.VMEM((16, ROWS, ROWS), f32),
            pltpu.VMEM((2, PAIR, 640), bf16),
        ],
        compiler_params=params,
        name="forward",
    )(attn_query, kx, lse_attn, index_query, index_weight)
    target, score = lax.psum((target, score), "narrow")
    offsets = jnp.arange(ROWS, dtype=jnp.int32)
    query_pos = block_order[place] * ROWS + offsets
    key_pos = (block_order[:, None] * ROWS + offsets[None, :]).reshape(8, 1, PAIR)
    causal = query_pos[None, :, None] >= key_pos
    diff = jnp.where(
        causal, jnp.exp(score - lse_index[None, :, None]) - target * (1.0 / HEADS), 0.0
    ).astype(bf16)
    u, dk = pl.pallas_call(
        backward,
        grid=(8,),
        out_shape=(sds((2048, ROWS), f32), sds((8, ROWS, PAIR), f32)),
        in_specs=[slab(2048, PAIR), slab(PAIR, 768), slab(ROWS, PAIR), whole(ROWS, 2048), whole(16, ROWS)],
        out_specs=(whole(2048, ROWS), slab(ROWS, PAIR)),
        scratch_shapes=[pltpu.VMEM((PAIR, 2048), bf16)],
        compiler_params=params,
        name="backward",
    )(logit, kx, diff, index_query, index_weight)
    u = u.reshape(16, ROWS, ROWS)
    heads = jnp.transpose(index_query.reshape(ROWS, 16, ROWS), (1, 0, 2)).astype(f32)
    d_weight = jnp.sum(heads * u, axis=2) * INDEX_SCALE
    d_query = jnp.transpose(u * (index_weight * INDEX_SCALE)[:, :, None], (1, 0, 2)).reshape(ROWS, 2048)
    dk = jnp.transpose(dk, (0, 2, 1)).reshape(2048, ROWS)
    d_key = lax.psum(lax.psum_scatter(dk, "wide", scatter_dimension=0, tiled=True), "narrow")
    return d_query, d_weight, d_key


def solution(mesh):
    in_specs = (
        P(("seq", "wide"), "narrow"),
        P(("seq", "wide"), None),
        P("narrow", ("seq", "wide")),
        P(("seq", "wide"), "narrow"),
        P(("seq", "wide"), None),
        P("narrow", ("seq", "wide")),
        P(("seq", "wide")),
        P("seq"),
    )
    out_specs = (
        P(("seq", "wide"), "narrow"),
        P("narrow", ("seq", "wide")),
        P(("seq", "wide"), None),
    )
    return jax.shard_map(body, mesh=mesh, in_specs=in_specs, out_specs=out_specs, check_vma=False)
```

```python
import jax
import jax.numpy as jnp
from jax import lax
from jax.experimental import pallas as pl
from jax.experimental.pallas import tpu as pltpu
from jax.sharding import PartitionSpec as P

HEADS = 128
LOG2E = 1.4426950408889634
ATTN_SCALE2 = 192.0 ** (-0.5) * LOG2E
INDEX_SCALE = 128.0 ** (-0.5)
ROWS = 128
PAIR = 256
STEPS = 8
NT = (((1,), (1,)), ((), ()))
NN = (((1,), (0,)), ((), ()))
f32 = jnp.float32
bf16 = jnp.bfloat16
MESH = pl.DeviceIdType.MESH


def twice(x):
    return jnp.concatenate([x, x], axis=1)


def target_sum(q_ref, kab, lse_b):
    group = 4
    total = None
    for g in range(16 // group):
        for par in range(2):
            parts = [
                q_ref[:, (g * group + i) * 1152 + par * 512 : (g * group + i) * 1152 + par * 512 + 640]
                for i in range(group)
            ]
            s = lax.dot_general(
                jnp.concatenate(parts, axis=0), kab[par], NT, preferred_element_type=f32
            )
            for i in range(group):
                h = (g * group + i) * 2 + par
                e = jnp.exp2(s[i * ROWS : (i + 1) * ROWS] * ATTN_SCALE2 - twice(lse_b[h]))
                total = e if total is None else total + e
    return total


def score_sum(iq_ref, ikey, w_b, keep):
    total = None
    for g in range(2):
        lhs = jnp.concatenate(
            [iq_ref[:, (g * 8 + i) * ROWS : (g * 8 + i + 1) * ROWS] for i in range(8)], axis=0
        )
        s = lax.dot_general(lhs, ikey, NT, preferred_element_type=f32)
        keep(g, s.astype(bf16))
        for i in range(8):
            e = jnp.maximum(s[i * ROWS : (i + 1) * ROWS], 0.0) * twice(w_b[g * 8 + i])
            total = e if total is None else total + e
    return total


def kernel(
    q_hbm, latent_ref, lse_ref, iq_ref, ikey_ref, weight_ref, lidx_ref, order_ref,
    dq_ref, dw_ref, dk_ref,
    q_ref, kbuf, kab, lse_b, w_b, lidx_b, wq, logit, part, r1, s2, r2, own2, dbuf, u, dkp, rd1, sd2, rd2, fin,
    q_sem, cross_sem, ring_send, ring_recv, mate_send, mate_recv,
    p1_send, p1_recv, p2_send, p2_recv, p3_send, p3_recv, d1_send, d1_recv, d2_send, d2_recv,
    fin_send, fin_recv,
):
    wide = lax.axis_index("wide")
    narrow = lax.axis_index("narrow")
    xh, z = wide // 8, wide % 8
    xl, core = narrow // 2, narrow % 2
    is_own = xh == core
    rows64 = pl.multiple_of(core * 64, 64)
    rows32 = pl.multiple_of(core * 64 + xl * 32, 32)
    away32 = pl.multiple_of(core * 64 + (1 - xl) * 32, 32)

    def at(a, b, c, e):
        return {"wide": a * 8 + b, "narrow": c * 2 + e}

    mate = at(xh, z, xl, 1 - core)
    across = at(xh, z, 1 - xl, core)
    others = (mate, across, at(xh, z, 1 - xl, 1 - core))
    right = at(xh, (z + 1) % 8, xl, core)
    left = at(xh, (z + 7) % 8, xl, core)
    cross = at(1 - xh, z, 1 - xl, core)
    owner_xl = jnp.where(is_own, xl, 1 - xl)

    def owner(d):
        return at(core, (z + d) % 8, owner_xl, xh)

    def place(k):
        return jnp.where(k % 2 == 1, (k + 1) // 2, (8 - k // 2) % 8)

    def remote(src, dst, send, recv, dev):
        return pltpu.make_async_remote_copy(
            src_ref=src, dst_ref=dst, send_sem=send, recv_sem=recv, device_id=dev, device_id_type=MESH
        )

    def cross_copy():
        return remote(kbuf.at[0, core], kbuf.at[0, core], cross_sem.at[0], cross_sem.at[1], cross)

    def left_copy(d):
        return remote(kbuf.at[d, core], kbuf.at[d + 1, core], ring_send.at[d], ring_recv.at[d + 1], left)

    def right_copy(d):
        return remote(
            kbuf.at[d, core], kbuf.at[(d + 7) % 8, core], ring_send.at[8 + d], ring_recv.at[(d + 7) % 8], right
        )

    def mate_copy(d, c):
        return remote(kbuf.at[d, c], kbuf.at[d, c], mate_send.at[d], mate_recv.at[d], mate)

    def p1_copy(k):
        src = part.at[k, :, pl.ds(pl.multiple_of((1 - core) * 64, 64), 64), :]
        return remote(src, r1.at[k], p1_send.at[k], p1_recv.at[k], mate)

    def p2_copy(k):
        return remote(s2.at[k], r2.at[k], p2_send.at[k], p2_recv.at[k], across)

    def p3_copy(k, r):
        block = dbuf.at[k, pl.ds(rows32, 32), :]
        return remote(block, block, p3_send.at[k, r], p3_recv.at[k, r], others[r])

    def d1_copy(k):
        return remote(dkp.at[k, 1 - core], rd1.at[k], d1_send.at[k], d1_recv.at[k], mate)

    def d2_copy(k):
        return remote(sd2.at[k], rd2.at[k], d2_send.at[k], d2_recv.at[k], owner(place(k)))

    def fin_copy(r):
        return remote(fin.at[narrow], fin.at[narrow], fin_send.at[r], fin_recv.at[r], others[r])

    q_copy = pltpu.make_async_copy(q_hbm, q_ref, q_sem)
    q_copy.start()

    barrier = pltpu.get_barrier_semaphore()
    for dev in others + (right, left, cross):
        pl.semaphore_signal(barrier, inc=1, device_id=dev, device_id_type=MESH)

    def greet(d, _):
        @pl.when(jnp.logical_or(d > 0, jnp.logical_not(is_own)))
        def _():
            pl.semaphore_signal(barrier, inc=1, device_id=owner(d), device_id_type=MESH)

        return 0

    lax.fori_loop(0, 8, greet, 0)
    kbuf[0, xh, :, 0:576] = latent_ref[...]
    kbuf[0, xh, :, 576:640] = jnp.zeros((ROWS, 64), bf16)
    kbuf[0, xh, :, 640:768] = ikey_ref[...]
    pl.semaphore_wait(barrier, jnp.where(is_own, 13, 14))

    @pl.when(is_own)
    def _():
        cross_copy().start()
        left_copy(0).start()
        right_copy(0).start()

    lse_t = jnp.transpose(lse_ref[...]) * LOG2E
    for h in range(32):
        lse_b[h] = jnp.broadcast_to(lse_t[:, h : h + 1], (ROWS, ROWS))
    w_t = jnp.transpose(weight_ref[...]) * INDEX_SCALE
    for j in range(16):
        w_b[j] = jnp.broadcast_to(w_t[:, j : j + 1], (ROWS, ROWS))
    lidx_b[...] = jnp.transpose(jnp.broadcast_to(lidx_ref[...], (ROWS, ROWS)))

    @pl.when(jnp.logical_not(is_own))
    def _():
        cross_copy().wait_recv()
        mate_copy(0, core).start()
        left_copy(0).start()
        right_copy(0).start()

    for j in range(16):
        x = jnp.transpose(iq_ref[:, j * ROWS : (j + 1) * ROWS].astype(f32))
        x = x * (weight_ref[j : j + 1, :] * INDEX_SCALE)
        hi = x.astype(bf16)
        wq[0:128, j * ROWS : (j + 1) * ROWS] = hi
        wq[128:256, j * ROWS : (j + 1) * ROWS] = (x - hi.astype(f32)).astype(bf16)
    u[...] = jnp.zeros_like(u)
    q_copy.wait()

    def key_gradient(k):
        d1_copy(k).wait_recv()
        total = (dkp[k, core] + rd1[k]).astype(bf16)
        here = jnp.logical_and(k == 0, is_own)

        @pl.when(here)
        def _():
            rd2[k] = total

        @pl.when(jnp.logical_not(here))
        def _():
            sd2[k] = total
            d2_copy(k).start()

    def step(k, _):
        d = place(k)

        @pl.when(k < STEPS)
        def _():
            @pl.when(jnp.logical_or(k > 0, is_own))
            def _():
                mate_copy(d, 1 - core).wait_recv()

            for c in range(2):
                block = kbuf[d, c]
                kab[0, c * ROWS : (c + 1) * ROWS] = block[:, 0:640]
                kab[1, c * ROWS : (c + 1) * ROWS] = jnp.concatenate(
                    [block[:, 576:640], block[:, 0:576]], axis=1
                )
            part[k, 0] = target_sum(q_ref, kab, lse_b)

        @pl.when(jnp.logical_and(k % 2 == 0, k < STEPS))
        def _():
            r = k // 2 + 1
            remote(
                kbuf.at[r, core], kbuf.at[r, core], ring_send.at[r], ring_recv.at[r], left
            ).wait_recv()
            mate_copy(r, core).start()

            @pl.when(jnp.logical_or(r < 3, jnp.logical_and(r == 3, core == 0)))
            def _():
                left_copy(r).start()

            @pl.when(r < 4)
            def _():
                e = 8 - r
                remote(
                    kbuf.at[e, core], kbuf.at[e, core], ring_send.at[8 + e], ring_recv.at[e], right
                ).wait_recv()
                mate_copy(e, core).start()

                @pl.when(jnp.logical_or(r < 3, core == 1))
                def _():
                    right_copy(e).start()

        @pl.when(jnp.logical_and(k >= 1, k <= STEPS))
        def _():
            b = k - 1
            p1_copy(b).wait_recv()
            far = pl.multiple_of((1 - xl) * 32, 32)
            near = pl.multiple_of(xl * 32, 32)
            for a in range(2):
                s2[b, a] = part[b, a, pl.ds(away32, 32), :] + r1[b, a, pl.ds(far, 32), :]
            p2_copy(b).start()
            for a in range(2):
                own2[a] = part[b, a, pl.ds(rows32, 32), :] + r1[b, a, pl.ds(near, 32), :]

        @pl.when(k >= 3)
        def _():
            key_gradient(k - 3)

        @pl.when(k < STEPS)
        def _():
            ikey = jnp.concatenate([kbuf[d, 0, :, 640:768], kbuf[d, 1, :, 640:768]], axis=0)

            def keep(g, x):
                logit[k, g * 1024 : (g + 1) * 1024] = x

            part[k, 1] = score_sum(iq_ref, ikey, w_b, keep)
            p1_copy(k).start()

        @pl.when(k >= 2)
        def _():
            b = k - 2
            for r in range(3):
                p3_copy(b, r).wait_recv()
            dd = place(b)
            diff = dbuf[b]
            md = jnp.concatenate(
                [
                    jnp.where(logit[b, j * ROWS : (j + 1) * ROWS] > 0, diff, jnp.zeros_like(diff))
                    for j in range(16)
                ],
                axis=0,
            )
            ikey = jnp.concatenate([kbuf[dd, 0, :, 640:768], kbuf[dd, 1, :, 640:768]], axis=0)
            both = lax.dot_general(wq[...], md, NN, preferred_element_type=f32)
            dkt = both[0:128] + both[128:256]
            dkp[b, 0] = dkt[:, 0:128]
            dkp[b, 1] = dkt[:, 128:256]
            d1_copy(b).start()
            u[...] += lax.dot_general(md, ikey, NN, preferred_element_type=f32)

        @pl.when(jnp.logical_and(k >= 1, k <= STEPS))
        def _():
            b = k - 1
            p2_copy(b).wait_recv()
            target = own2[0] + r2[b, 0]
            score = own2[1] + r2[b, 1]
            lidx = lidx_b[pl.ds(rows32, 32), :]
            zs = (z + place(b)) % 8
            row = order_ref[wide] * ROWS + rows32 + lax.broadcasted_iota(jnp.int32, (32, ROWS), 0)
            lane = lax.broadcasted_iota(jnp.int32, (32, ROWS), 1)
            causal = jnp.concatenate(
                [row >= order_ref[h * 8 + zs] * ROWS + lane for h in range(2)], axis=1
            )
            diff = jnp.exp(score - twice(lidx)) - target * (1.0 / HEADS)
            dbuf[b, pl.ds(rows32, 32), :] = jnp.where(causal, diff, 0.0).astype(bf16)
            for r in range(3):
                p3_copy(b, r).start()

        return 0

    lax.fori_loop(0, STEPS + 2, step, 0)

    sums = []
    for j in range(16):
        uj = u[j * ROWS : (j + 1) * ROWS, :]
        cols = slice(j * ROWS, (j + 1) * ROWS)
        dq_ref[:, cols] = uj * w_b[j]
        prod = jnp.transpose(uj * iq_ref[:, cols].astype(f32))
        sums.append(jnp.sum(prod, axis=0, keepdims=True) * INDEX_SCALE)
        if j == 3:
            key_gradient(STEPS - 1)
    dw_ref[...] = jnp.concatenate(sums, axis=0)

    total = None
    for k in range(STEPS):
        if k == 0:

            @pl.when(jnp.logical_not(is_own))
            def _():
                d2_copy(0).wait_recv()

        else:
            d2_copy(k).wait_recv()
        total = rd2[k].astype(f32) if total is None else total + rd2[k].astype(f32)
    fin[narrow] = total.astype(bf16)
    for r in range(3):
        fin_copy(r).start()
    for r in range(3):
        fin_copy(r).wait_recv()
    total = (fin[0].astype(f32) + fin[1].astype(f32)) + (fin[2].astype(f32) + fin[3].astype(f32))
    dk_ref[...] = jnp.transpose(total)

    for r in range(3):
        fin_copy(r).wait_send()

    @pl.when(is_own)
    def _():
        cross_copy().wait_send()

    def drain(k, _):
        p1_copy(k).wait_send()
        p2_copy(k).wait_send()
        for r in range(3):
            p3_copy(k, r).wait_send()
        d1_copy(k).wait_send()

        @pl.when(jnp.logical_or(k > 0, jnp.logical_not(is_own)))
        def _():
            d2_copy(k).wait_send()
            mate_copy(k, core).wait_send()

        @pl.when(jnp.logical_or(k < 3, jnp.logical_and(k == 3, core == 0)))
        def _():
            left_copy(k).wait_send()

        @pl.when(jnp.logical_or(k < 3, jnp.logical_and(k == 3, core == 1)))
        def _():
            right_copy((8 - k) % 8).wait_send()

        return 0

    lax.fori_loop(0, STEPS, drain, 0)


def body(
    attn_query, key_latent, lse_attn, index_query, index_key, index_weight, lse_index, block_order
):
    sds = jax.ShapeDtypeStruct
    vm = pl.BlockSpec(memory_space=pltpu.VMEM)
    dma = pltpu.SemaphoreType.DMA
    return pl.pallas_call(
        kernel,
        out_shape=(sds((ROWS, 2048), f32), sds((16, ROWS), f32), sds((ROWS, ROWS), f32)),
        in_specs=[pl.BlockSpec(memory_space=pl.ANY)]
        + [vm] * 6
        + [pl.BlockSpec(memory_space=pltpu.SMEM)],
        out_specs=(vm, vm, vm),
        scratch_shapes=[
            pltpu.VMEM((ROWS, 18432), bf16),
            pltpu.VMEM((8, 2, ROWS, 768), bf16),
            pltpu.VMEM((2, PAIR, 640), bf16),
            pltpu.VMEM((32, ROWS, ROWS), f32),
            pltpu.VMEM((16, ROWS, ROWS), f32),
            pltpu.VMEM((ROWS, ROWS), f32),
            pltpu.VMEM((PAIR, 2048), bf16),
            pltpu.VMEM((STEPS, 2048, PAIR), bf16),
            pltpu.VMEM((STEPS, 2, ROWS, PAIR), f32),
            pltpu.VMEM((STEPS, 2, 64, PAIR), f32),
            pltpu.VMEM((STEPS, 2, 32, PAIR), f32),
            pltpu.VMEM((STEPS, 2, 32, PAIR), f32),
            pltpu.VMEM((2, 32, PAIR), f32),
            pltpu.VMEM((STEPS, ROWS, PAIR), bf16),
            pltpu.VMEM((2048, ROWS), f32),
            pltpu.VMEM((STEPS, 2, ROWS, ROWS), f32),
            pltpu.VMEM((STEPS, ROWS, ROWS), f32),
            pltpu.VMEM((STEPS, ROWS, ROWS), bf16),
            pltpu.VMEM((STEPS, ROWS, ROWS), bf16),
            pltpu.VMEM((4, ROWS, ROWS), bf16),
            dma(()),
            dma((2,)),
            dma((16,)),
            dma((8,)),
            dma((8,)),
            dma((8,)),
            dma((STEPS,)),
            dma((STEPS,)),
            dma((STEPS,)),
            dma((STEPS,)),
            dma((STEPS, 3)),
            dma((STEPS, 3)),
            dma((STEPS,)),
            dma((STEPS,)),
            dma((STEPS,)),
            dma((STEPS,)),
            dma((3,)),
            dma((3,)),
        ],
        compiler_params=pltpu.CompilerParams(
            vmem_limit_bytes=56 << 20, collective_id=0, has_side_effects=True
        ),
        name="indexer",
    )(
        attn_query, key_latent, lse_attn, index_query, index_key, index_weight,
        lse_index.reshape(1, ROWS), block_order,
    )


def solution(mesh):
    in_specs = (
        P(("seq", "wide"), "narrow"),
        P(("seq", "wide"), None),
        P("narrow", ("seq", "wide")),
        P(("seq", "wide"), "narrow"),
        P(("seq", "wide"), None),
        P("narrow", ("seq", "wide")),
        P(("seq", "wide")),
        P("seq"),
    )
    out_specs = (
        P(("seq", "wide"), "narrow"),
        P("narrow", ("seq", "wide")),
        P(("seq", "wide"), None),
    )
    return jax.shard_map(body, mesh=mesh, in_specs=in_specs, out_specs=out_specs, check_vma=False)
```

```python
import jax
import jax.numpy as jnp
from jax import lax
from jax.experimental import pallas as pl
from jax.experimental.pallas import tpu as pltpu
from jax.sharding import PartitionSpec as P

HEADS = 128
LOG2E = 1.4426950408889634
ATTN_SCALE2 = 192.0 ** (-0.5) * LOG2E
INDEX_SCALE = 128.0 ** (-0.5)
ROWS = 128
PAIR = 256
STEPS = 8
LAG = 4
NT = (((1,), (1,)), ((), ()))
NN = (((1,), (0,)), ((), ()))
f32 = jnp.float32
bf16 = jnp.bfloat16
MESH = pl.DeviceIdType.MESH


def twice(x):
    return jnp.concatenate([x, x], axis=1)


def target_sum(q_ref, kab, lse_b):
    group = 4
    total = None
    for g in range(16 // group):
        for par in range(2):
            parts = [
                q_ref[:, (g * group + i) * 1152 + par * 512 : (g * group + i) * 1152 + par * 512 + 640]
                for i in range(group)
            ]
            s = lax.dot_general(
                jnp.concatenate(parts, axis=0), kab[par], NT, preferred_element_type=f32
            )
            for i in range(group):
                h = (g * group + i) * 2 + par
                e = jnp.exp2(s[i * ROWS : (i + 1) * ROWS] * ATTN_SCALE2 - twice(lse_b[h]))
                total = e if total is None else total + e
    return total


def score_sum(iq_ref, ikey, w_b, keep):
    total = None
    for g in range(2):
        lhs = jnp.concatenate(
            [iq_ref[:, (g * 8 + i) * ROWS : (g * 8 + i + 1) * ROWS] for i in range(8)], axis=0
        )
        s = lax.dot_general(lhs, ikey, NT, preferred_element_type=f32)
        keep(g, s.astype(bf16))
        for i in range(8):
            e = jnp.maximum(s[i * ROWS : (i + 1) * ROWS], 0.0) * twice(w_b[g * 8 + i])
            total = e if total is None else total + e
    return total


def kernel(
    q_hbm, latent_ref, lse_ref, iq_ref, ikey_ref, weight_ref, lidx_ref, order_ref,
    u, total_ref,
    q_ref, kbuf, kab, lse_b, w_b, lidx_b, wq, logit, part, r1, s2, r2, own2, dbuf, dkp, rd1, sd2, rd2, fin,
    q_sem, cross_sem, ring_send, ring_recv, mate_send, mate_recv,
    p1_send, p1_recv, p2_send, p2_recv, p3_send, p3_recv, d1_send, d1_recv, d2_send, d2_recv,
    fin_send, fin_recv,
):
    wide = lax.axis_index("wide")
    narrow = lax.axis_index("narrow")
    xh, z = wide // 8, wide % 8
    xl, core = narrow // 2, narrow % 2
    is_own = xh == core
    rows64 = pl.multiple_of(core * 64, 64)
    rows32 = pl.multiple_of(core * 64 + xl * 32, 32)
    away32 = pl.multiple_of(core * 64 + (1 - xl) * 32, 32)

    def at(a, b, c, e):
        return {"wide": a * 8 + b, "narrow": c * 2 + e}

    mate = at(xh, z, xl, 1 - core)
    across = at(xh, z, 1 - xl, core)
    others = (mate, across, at(xh, z, 1 - xl, 1 - core))
    right = at(xh, (z + 1) % 8, xl, core)
    left = at(xh, (z + 7) % 8, xl, core)
    cross = at(1 - xh, z, 1 - xl, core)
    owner_xl = jnp.where(is_own, xl, 1 - xl)

    def owner(d):
        return at(core, (z + d) % 8, owner_xl, core)

    def place(k):
        return jnp.where(k % 2 == 1, (k + 1) // 2, (8 - k // 2) % 8)

    def remote(src, dst, send, recv, dev):
        return pltpu.make_async_remote_copy(
            src_ref=src, dst_ref=dst, send_sem=send, recv_sem=recv, device_id=dev, device_id_type=MESH
        )

    def cross_copy():
        return remote(kbuf.at[0, core], kbuf.at[0, core], cross_sem.at[0], cross_sem.at[1], cross)

    def left_copy(d):
        return remote(kbuf.at[d, core], kbuf.at[d + 1, core], ring_send.at[d], ring_recv.at[d + 1], left)

    def right_copy(d):
        return remote(
            kbuf.at[d, core], kbuf.at[(d + 7) % 8, core], ring_send.at[8 + d], ring_recv.at[(d + 7) % 8], right
        )

    def mate_copy(d, c):
        return remote(kbuf.at[d, c], kbuf.at[d, c], mate_send.at[d], mate_recv.at[d], mate)

    def p1_copy(k):
        src = part.at[k, :, pl.ds(pl.multiple_of((1 - core) * 64, 64), 64), :]
        return remote(src, r1.at[k], p1_send.at[k], p1_recv.at[k], mate)

    def p2_copy(k):
        return remote(s2.at[k], r2.at[k], p2_send.at[k], p2_recv.at[k], across)

    def p3_copy(k, r):
        block = dbuf.at[k, pl.ds(rows32, 32), :]
        return remote(block, block, p3_send.at[k, r], p3_recv.at[k, r], others[r])

    def d1_copy(k):
        return remote(dkp.at[k, 1 - core], rd1.at[k], d1_send.at[k], d1_recv.at[k], mate)

    def d2_copy(k):
        kind = jnp.where(is_own, 0, 1)
        return remote(
            sd2.at[k], rd2.at[kind, k], d2_send.at[k], d2_recv.at[kind, k], owner(place(k))
        )

    def d2_arrival(kind, k):
        return remote(sd2.at[k], rd2.at[kind, k], d2_send.at[k], d2_recv.at[kind, k], owner(0))

    def fin_copy(r):
        return remote(fin.at[xl], fin.at[xl], fin_send.at[r], fin_recv.at[r], others[r])

    q_copy = pltpu.make_async_copy(q_hbm, q_ref, q_sem)
    barrier = pltpu.get_barrier_semaphore()
    for dev in others + (right, left, cross):
        pl.semaphore_signal(barrier, inc=1, device_id=dev, device_id_type=MESH)
    q_copy.start()
    for i in range(4):
        kbuf[0, xh, :, i * ROWS : (i + 1) * ROWS] = jnp.transpose(
            latent_ref[i * ROWS : (i + 1) * ROWS, :].astype(f32)
        ).astype(bf16)
    last = jnp.transpose(latent_ref[512:576, :].astype(f32)).astype(bf16)
    kbuf[0, xh, :, 512:640] = jnp.concatenate([last, jnp.zeros((ROWS, 64), bf16)], axis=1)
    kbuf[0, xh, :, 640:768] = ikey_ref[...]
    pl.semaphore_wait(barrier, 6)

    @pl.when(is_own)
    def _():
        cross_copy().start()
        left_copy(0).start()
        right_copy(0).start()

    lse_t = jnp.transpose(lse_ref[...]) * LOG2E
    for h in range(32):
        lse_b[h] = jnp.broadcast_to(lse_t[:, h : h + 1], (ROWS, ROWS))
    w_t = jnp.transpose(weight_ref[...]) * INDEX_SCALE
    for j in range(16):
        w_b[j] = jnp.broadcast_to(w_t[:, j : j + 1], (ROWS, ROWS))
    lidx_b[...] = jnp.transpose(jnp.broadcast_to(lidx_ref[...], (ROWS, ROWS)))

    @pl.when(jnp.logical_not(is_own))
    def _():
        cross_copy().wait_recv()
        mate_copy(0, core).start()
        left_copy(0).start()
        right_copy(0).start()

    for j in range(16):
        x = jnp.transpose(iq_ref[:, j * ROWS : (j + 1) * ROWS].astype(f32))
        x = x * (weight_ref[j : j + 1, :] * INDEX_SCALE)
        hi = x.astype(bf16)
        wq[0:128, j * ROWS : (j + 1) * ROWS] = hi
        wq[128:256, j * ROWS : (j + 1) * ROWS] = (x - hi.astype(f32)).astype(bf16)
    u[...] = jnp.zeros_like(u)
    q_copy.wait()

    def key_gradient(k):
        d1_copy(k).wait_recv()
        total = (dkp[k, core] + rd1[k]).astype(bf16)
        here = jnp.logical_and(k == 0, is_own)

        @pl.when(here)
        def _():
            rd2[0, 0] = total

        @pl.when(jnp.logical_not(here))
        def _():
            sd2[k] = total
            d2_copy(k).start()

    def pump(k):
        r = k // 2 + 1
        remote(
            kbuf.at[r, core], kbuf.at[r, core], ring_send.at[r], ring_recv.at[r], left
        ).wait_recv()
        mate_copy(r, core).start()

        @pl.when(jnp.logical_or(r < 3, jnp.logical_and(r == 3, core == 0)))
        def _():
            left_copy(r).start()

        @pl.when(r < 4)
        def _():
            e = 8 - r
            remote(
                kbuf.at[e, core], kbuf.at[e, core], ring_send.at[8 + e], ring_recv.at[e], right
            ).wait_recv()
            mate_copy(e, core).start()

            @pl.when(jnp.logical_or(r < 3, core == 1))
            def _():
                right_copy(e).start()

    def step(k, _):
        d = place(k)

        @pl.when(k < STEPS)
        def _():
            @pl.when(jnp.logical_or(k > 0, is_own))
            def _():
                mate_copy(d, 1 - core).wait_recv()

            for c in range(2):
                block = kbuf[d, c]
                kab[0, c * ROWS : (c + 1) * ROWS] = block[:, 0:640]
                kab[1, c * ROWS : (c + 1) * ROWS] = jnp.concatenate(
                    [block[:, 576:640], block[:, 0:576]], axis=1
                )
            part[k, 0] = target_sum(q_ref, kab, lse_b)

        @pl.when(jnp.logical_and(jnp.logical_and(k % 2 == 0, k > 0), k < STEPS))
        def _():
            pump(k)

        @pl.when(jnp.logical_and(k >= 1, k <= STEPS))
        def _():
            b = k - 1
            p1_copy(b).wait_recv()
            far = pl.multiple_of((1 - xl) * 32, 32)
            near = pl.multiple_of(xl * 32, 32)
            for a in range(2):
                s2[b, a] = part[b, a, pl.ds(away32, 32), :] + r1[b, a, pl.ds(far, 32), :]
            p2_copy(b).start()
            for a in range(2):
                own2[b, a] = part[b, a, pl.ds(rows32, 32), :] + r1[b, a, pl.ds(near, 32), :]

        @pl.when(k > LAG)
        def _():
            key_gradient(k - LAG - 1)

        @pl.when(k < STEPS)
        def _():
            ikey = jnp.concatenate([kbuf[d, 0, :, 640:768], kbuf[d, 1, :, 640:768]], axis=0)

            def keep(g, x):
                logit[k, g * 1024 : (g + 1) * 1024] = x

            part[k, 1] = score_sum(iq_ref, ikey, w_b, keep)
            p1_copy(k).start()

        @pl.when(k == 0)
        def _():
            pump(k)

        @pl.when(k >= LAG)
        def _():
            b = k - LAG
            for r in range(3):
                p3_copy(b, r).wait_recv()
            dd = place(b)
            diff = dbuf[b]
            md = jnp.concatenate(
                [
                    jnp.where(logit[b, j * ROWS : (j + 1) * ROWS] > 0, diff, jnp.zeros_like(diff))
                    for j in range(16)
                ],
                axis=0,
            )
            ikey = jnp.concatenate([kbuf[dd, 0, :, 640:768], kbuf[dd, 1, :, 640:768]], axis=0)
            both = lax.dot_general(wq[...], md, NN, preferred_element_type=f32)
            dkt = both[0:128] + both[128:256]
            dkp[b, 0] = dkt[:, 0:128]
            dkp[b, 1] = dkt[:, 128:256]
            d1_copy(b).start()
            u[...] += lax.dot_general(md, ikey, NN, preferred_element_type=f32)

        @pl.when(jnp.logical_and(k >= 2, k <= STEPS + 1))
        def _():
            b = k - 2
            p2_copy(b).wait_recv()
            target = own2[b, 0] + r2[b, 0]
            score = own2[b, 1] + r2[b, 1]
            lidx = lidx_b[pl.ds(rows32, 32), :]
            zs = (z + place(b)) % 8
            row = order_ref[wide] * ROWS + rows32 + lax.broadcasted_iota(jnp.int32, (32, ROWS), 0)
            lane = lax.broadcasted_iota(jnp.int32, (32, ROWS), 1)
            causal = jnp.concatenate(
                [row >= order_ref[h * 8 + zs] * ROWS + lane for h in range(2)], axis=1
            )
            diff = jnp.exp(score - twice(lidx)) - target * (1.0 / HEADS)
            dbuf[b, pl.ds(rows32, 32), :] = jnp.where(causal, diff, 0.0).astype(bf16)
            for r in range(3):
                p3_copy(b, r).start()

        return 0

    lax.fori_loop(0, STEPS + LAG, step, 0)
    key_gradient(STEPS - 1)

    @pl.when(is_own)
    def _():
        total = None
        for k in range(STEPS):
            for kind in range(2):
                if k + kind > 0:
                    d2_arrival(kind, k).wait_recv()
                x = rd2[kind, k].astype(f32)
                total = x if total is None else total + x
        fin[xl] = total.astype(bf16)
        for r in range(3):
            fin_copy(r).start()
        fin_copy(1).wait_recv()

    @pl.when(jnp.logical_not(is_own))
    def _():
        fin_copy(0).wait_recv()
        fin_copy(2).wait_recv()

    total_ref[...] = fin[0].astype(f32) + fin[1].astype(f32)

    @pl.when(is_own)
    def _():
        for r in range(3):
            fin_copy(r).wait_send()
        cross_copy().wait_send()

    def drain(k, _):
        p1_copy(k).wait_send()
        p2_copy(k).wait_send()
        for r in range(3):
            p3_copy(k, r).wait_send()
        d1_copy(k).wait_send()

        @pl.when(jnp.logical_or(k > 0, jnp.logical_not(is_own)))
        def _():
            d2_copy(k).wait_send()
            mate_copy(k, core).wait_send()

        @pl.when(jnp.logical_or(k < 3, jnp.logical_and(k == 3, core == 0)))
        def _():
            left_copy(k).wait_send()

        @pl.when(jnp.logical_or(k < 3, jnp.logical_and(k == 3, core == 1)))
        def _():
            right_copy((8 - k) % 8).wait_send()

        return 0

    lax.fori_loop(0, STEPS, drain, 0)


def finish(u_ref, total_ref, iq_ref, weight_ref, dq_ref, dw_ref, dk_ref):
    g = pl.program_id(0)

    @pl.when(g == 0)
    def _():
        dk_ref[...] = jnp.transpose(total_ref[...])

    w_t = jnp.transpose(weight_ref[...]) * INDEX_SCALE
    sums = []
    for j in range(8):
        uj = u_ref[j * ROWS : (j + 1) * ROWS, :]
        cols = slice(j * ROWS, (j + 1) * ROWS)
        dq_ref[:, cols] = uj * jnp.broadcast_to(w_t[:, j : j + 1], (ROWS, ROWS))
        prod = jnp.transpose(uj * iq_ref[:, cols].astype(f32))
        sums.append(jnp.sum(prod, axis=0, keepdims=True) * INDEX_SCALE)
    dw_ref[...] = jnp.concatenate(sums, axis=0)


def body(
    attn_query, key_latent, lse_attn, index_query, index_key, index_weight, lse_index, block_order
):
    sds = jax.ShapeDtypeStruct
    vm = pl.BlockSpec(memory_space=pltpu.VMEM)
    dma = pltpu.SemaphoreType.DMA
    u, total = pl.pallas_call(
        kernel,
        out_shape=(sds((2048, ROWS), f32), sds((ROWS, ROWS), f32)),
        in_specs=[pl.BlockSpec(memory_space=pl.ANY)]
        + [vm] * 6
        + [pl.BlockSpec(memory_space=pltpu.SMEM)],
        out_specs=(vm, vm),
        scratch_shapes=[
            pltpu.VMEM((ROWS, 18432), bf16),
            pltpu.VMEM((8, 2, ROWS, 768), bf16),
            pltpu.VMEM((2, PAIR, 640), bf16),
            pltpu.VMEM((32, ROWS, ROWS), f32),
            pltpu.VMEM((16, ROWS, ROWS), f32),
            pltpu.VMEM((ROWS, ROWS), f32),
            pltpu.VMEM((PAIR, 2048), bf16),
            pltpu.VMEM((STEPS, 2048, PAIR), bf16),
            pltpu.VMEM((STEPS, 2, ROWS, PAIR), f32),
            pltpu.VMEM((STEPS, 2, 64, PAIR), f32),
            pltpu.VMEM((STEPS, 2, 32, PAIR), f32),
            pltpu.VMEM((STEPS, 2, 32, PAIR), f32),
            pltpu.VMEM((STEPS, 2, 32, PAIR), f32),
            pltpu.VMEM((STEPS, ROWS, PAIR), bf16),
            pltpu.VMEM((STEPS, 2, ROWS, ROWS), f32),
            pltpu.VMEM((STEPS, ROWS, ROWS), f32),
            pltpu.VMEM((STEPS, ROWS, ROWS), bf16),
            pltpu.VMEM((2, STEPS, ROWS, ROWS), bf16),
            pltpu.VMEM((2, ROWS, ROWS), bf16),
            dma(()),
            dma((2,)),
            dma((16,)),
            dma((8,)),
            dma((8,)),
            dma((8,)),
            dma((STEPS,)),
            dma((STEPS,)),
            dma((STEPS,)),
            dma((STEPS,)),
            dma((STEPS, 3)),
            dma((STEPS, 3)),
            dma((STEPS,)),
            dma((STEPS,)),
            dma((STEPS,)),
            dma((2, STEPS)),
            dma((3,)),
            dma((3,)),
        ],
        compiler_params=pltpu.CompilerParams(
            vmem_limit_bytes=56 << 20, collective_id=0, has_side_effects=True
        ),
        name="indexer",
    )(
        attn_query, jnp.transpose(key_latent), lse_attn, index_query, index_key, index_weight,
        lse_index.reshape(1, ROWS), block_order,
    )
    return pl.pallas_call(
        finish,
        grid=(2,),
        out_shape=(sds((ROWS, 2048), f32), sds((16, ROWS), f32), sds((ROWS, ROWS), f32)),
        in_specs=[
            pl.BlockSpec((1024, ROWS), lambda g: (g, 0)),
            pl.BlockSpec((ROWS, ROWS), lambda g: (0, 0)),
            pl.BlockSpec((ROWS, 1024), lambda g: (0, g)),
            pl.BlockSpec((8, ROWS), lambda g: (g, 0)),
        ],
        out_specs=(
            pl.BlockSpec((ROWS, 1024), lambda g: (0, g)),
            pl.BlockSpec((8, ROWS), lambda g: (g, 0)),
            pl.BlockSpec((ROWS, ROWS), lambda g: (0, 0)),
        ),
        name="finish",
    )(u, total, index_query, index_weight)


def solution(mesh):
    in_specs = (
        P(("seq", "wide"), "narrow"),
        P(("seq", "wide"), None),
        P("narrow", ("seq", "wide")),
        P(("seq", "wide"), "narrow"),
        P(("seq", "wide"), None),
        P("narrow", ("seq", "wide")),
        P(("seq", "wide")),
        P("seq"),
    )
    out_specs = (
        P(("seq", "wide"), "narrow"),
        P("narrow", ("seq", "wide")),
        P(("seq", "wide"), None),
    )
    return jax.shard_map(body, mesh=mesh, in_specs=in_specs, out_specs=out_specs, check_vma=False)
```

```python
import jax
import jax.numpy as jnp
from jax import lax
from jax.experimental import pallas as pl
from jax.experimental.pallas import tpu as pltpu
from jax.sharding import PartitionSpec as P

HEADS = 128
LOG2E = 1.4426950408889634
ATTN_SCALE2 = 192.0 ** (-0.5) * LOG2E
INDEX_SCALE = 128.0 ** (-0.5)
ROWS = 128
PAIR = 256
STEPS = 8
NT = (((1,), (1,)), ((), ()))
NN = (((1,), (0,)), ((), ()))
f32 = jnp.float32
bf16 = jnp.bfloat16
MESH = pl.DeviceIdType.MESH


def twice(x):
    return jnp.concatenate([x, x], axis=1)


def target_sum(q_ref, kab, lse_b):
    group = 4
    total = None
    for g in range(16 // group):
        for par in range(2):
            parts = [
                q_ref[:, (g * group + i) * 1152 + par * 512 : (g * group + i) * 1152 + par * 512 + 640]
                for i in range(group)
            ]
            s = lax.dot_general(
                jnp.concatenate(parts, axis=0), kab[par], NT, preferred_element_type=f32
            )
            for i in range(group):
                h = (g * group + i) * 2 + par
                e = jnp.exp2(s[i * ROWS : (i + 1) * ROWS] * ATTN_SCALE2 - twice(lse_b[h]))
                total = e if total is None else total + e
    return total


def score_sum(iq_ref, ikey, w_b, keep):
    total = None
    for g in range(2):
        lhs = jnp.concatenate(
            [iq_ref[:, (g * 8 + i) * ROWS : (g * 8 + i + 1) * ROWS] for i in range(8)], axis=0
        )
        s = lax.dot_general(lhs, ikey, NT, preferred_element_type=f32)
        keep(g, s.astype(bf16))
        for i in range(8):
            e = jnp.maximum(s[i * ROWS : (i + 1) * ROWS], 0.0) * twice(w_b[g * 8 + i])
            total = e if total is None else total + e
    return total


def kernel(
    q_hbm, latent_ref, lse_ref, iq_hbm, ikey_ref, weight_ref, lidx_ref, order_ref,
    dq_ref, dw_ref, dk_ref,
    u, dq_v, iq_ref, q_ref, kbuf, kab, lse_b, w_b, lidx_b, wq, logit, part, r1, s2, r2, own2, dbuf, dkp, rd1, sd2, rd2, fin,
    q_sem, iq_sem, dq_sem, cross_sem, ring_send, ring_recv, mate_send, mate_recv,
    p1_send, p1_recv, p2_send, p2_recv, p3_send, p3_recv, d1_send, d1_recv, d2_send, d2_recv,
    fin_send, fin_recv,
):
    wide = lax.axis_index("wide")
    narrow = lax.axis_index("narrow")
    xh, z = wide // 8, wide % 8
    xl, core = narrow // 2, narrow % 2
    is_own = xh == core
    rows64 = pl.multiple_of(core * 64, 64)
    rows32 = pl.multiple_of(core * 64 + xl * 32, 32)
    away32 = pl.multiple_of(core * 64 + (1 - xl) * 32, 32)

    def at(a, b, c, e):
        return {"wide": a * 8 + b, "narrow": c * 2 + e}

    mate = at(xh, z, xl, 1 - core)
    across = at(xh, z, 1 - xl, core)
    others = (mate, across, at(xh, z, 1 - xl, 1 - core))
    right = at(xh, (z + 1) % 8, xl, core)
    left = at(xh, (z + 7) % 8, xl, core)
    cross = at(1 - xh, z, 1 - xl, core)

    def pair(k, h):
        r = (k + 1) // 2
        d = jnp.where(h == 0, r, (8 - r) % 8)
        c = jnp.where((k + 1) % 8 < 2, h, jnp.where(k % 2 == 1, xh, 1 - xh))
        return d, c

    def remote(src, dst, send, recv, dev):
        return pltpu.make_async_remote_copy(
            src_ref=src, dst_ref=dst, send_sem=send, recv_sem=recv, device_id=dev, device_id_type=MESH
        )

    def cross_copy():
        return remote(kbuf.at[0, core], kbuf.at[0, core], cross_sem.at[0], cross_sem.at[1], cross)

    def left_copy(d):
        return remote(kbuf.at[d, core], kbuf.at[d + 1, core], ring_send.at[d], ring_recv.at[d + 1], left)

    def right_copy(d):
        return remote(
            kbuf.at[d, core], kbuf.at[(d + 7) % 8, core], ring_send.at[8 + d], ring_recv.at[(d + 7) % 8], right
        )

    def mate_copy(d, c):
        return remote(kbuf.at[d, c], kbuf.at[d, c], mate_send.at[d], mate_recv.at[d], mate)

    def p1_copy(k):
        src = part.at[k, :, pl.ds(pl.multiple_of((1 - core) * 64, 64), 64), :]
        return remote(src, r1.at[k], p1_send.at[k], p1_recv.at[k], mate)

    def p2_copy(k):
        return remote(s2.at[k], r2.at[k], p2_send.at[k], p2_recv.at[k], across)

    def p3_copy(k, r):
        block = dbuf.at[k, pl.ds(rows32, 32), :]
        return remote(block, block, p3_send.at[k, r], p3_recv.at[k, r], others[r])

    def d1_copy(k):
        return remote(dkp.at[k, 1 - core], rd1.at[k], d1_send.at[k], d1_recv.at[k], mate)

    def d2_copy(k):
        d, c = pair(k, core)
        kind = jnp.where(c == xh, 0, 1)
        dev = at(c, (z + d) % 8, jnp.where(c == xh, xl, 1 - xl), c)
        return remote(sd2.at[k], rd2.at[kind, d], d2_send.at[k], d2_recv.at[kind, d], dev)

    def d2_arrival(kind, d):
        return remote(sd2.at[d], rd2.at[kind, d], d2_send.at[d], d2_recv.at[kind, d], mate)

    def fin_copy(r):
        return remote(fin.at[xl], fin.at[xl], fin_send.at[r], fin_recv.at[r], others[r])

    q_copy = pltpu.make_async_copy(q_hbm, q_ref, q_sem)
    iq_copy = pltpu.make_async_copy(iq_hbm, iq_ref, iq_sem)
    dq_copy = pltpu.make_async_copy(dq_v, dq_ref, dq_sem)
    barrier = pltpu.get_barrier_semaphore()
    for dev in others + (right, left, cross):
        pl.semaphore_signal(barrier, inc=1, device_id=dev, device_id_type=MESH)
    iq_copy.start()
    q_copy.start()
    for i in range(4):
        kbuf[0, xh, :, i * ROWS : (i + 1) * ROWS] = jnp.transpose(
            latent_ref[i * ROWS : (i + 1) * ROWS, :].astype(f32)
        ).astype(bf16)
    last = jnp.transpose(latent_ref[512:576, :].astype(f32)).astype(bf16)
    kbuf[0, xh, :, 512:640] = jnp.concatenate([last, jnp.zeros((ROWS, 64), bf16)], axis=1)
    kbuf[0, xh, :, 640:768] = ikey_ref[...]
    pl.semaphore_wait(barrier, 6)

    @pl.when(is_own)
    def _():
        cross_copy().start()
        left_copy(0).start()
        right_copy(0).start()

    lse_t = jnp.transpose(lse_ref[...]) * LOG2E
    for h in range(32):
        lse_b[h] = jnp.broadcast_to(lse_t[:, h : h + 1], (ROWS, ROWS))
    w_t = jnp.transpose(weight_ref[...]) * INDEX_SCALE
    for j in range(16):
        w_b[j] = jnp.broadcast_to(w_t[:, j : j + 1], (ROWS, ROWS))
    lidx_b[...] = jnp.transpose(jnp.broadcast_to(lidx_ref[...], (ROWS, ROWS)))

    @pl.when(jnp.logical_not(is_own))
    def _():
        cross_copy().wait_recv()
        mate_copy(0, core).start()
        left_copy(0).start()
        right_copy(0).start()

    iq_copy.wait()
    for j in range(16):
        x = jnp.transpose(iq_ref[:, j * ROWS : (j + 1) * ROWS].astype(f32))
        x = x * (weight_ref[j : j + 1, :] * INDEX_SCALE)
        hi = x.astype(bf16)
        wq[0:128, j * ROWS : (j + 1) * ROWS] = hi
        wq[128:256, j * ROWS : (j + 1) * ROWS] = (x - hi.astype(f32)).astype(bf16)
    u[...] = jnp.zeros_like(u)

    def key_gradient(k):
        d1_copy(k).wait_recv()
        total = (dkp[k, core] + rd1[k]).astype(bf16)
        here = jnp.logical_and(k == 0, is_own)

        @pl.when(here)
        def _():
            rd2[0, 0] = total

        @pl.when(jnp.logical_not(here))
        def _():
            sd2[k] = total
            d2_copy(k).start()

    def stage1(b):
        p1_copy(b).wait_recv()
        far = pl.multiple_of((1 - xl) * 32, 32)
        near = pl.multiple_of(xl * 32, 32)
        for a in range(2):
            s2[b, a] = part[b, a, pl.ds(away32, 32), :] + r1[b, a, pl.ds(far, 32), :]
        p2_copy(b).start()
        for a in range(2):
            own2[b, a] = part[b, a, pl.ds(rows32, 32), :] + r1[b, a, pl.ds(near, 32), :]

    def stage2(b):
        p2_copy(b).wait_recv()
        target = own2[b, 0] + r2[b, 0]
        score = own2[b, 1] + r2[b, 1]
        lidx = lidx_b[pl.ds(rows32, 32), :]
        row = order_ref[wide] * ROWS + rows32 + lax.broadcasted_iota(jnp.int32, (32, ROWS), 0)
        lane = lax.broadcasted_iota(jnp.int32, (32, ROWS), 1)
        causal = []
        for h in range(2):
            d, c = pair(b, h)
            causal.append(row >= order_ref[c * 8 + (z + d) % 8] * ROWS + lane)
        diff = jnp.exp(score - twice(lidx)) - target * (1.0 / HEADS)
        diff = jnp.where(jnp.concatenate(causal, axis=1), diff, 0.0)
        dbuf[b, pl.ds(rows32, 32), :] = diff.astype(bf16)
        for r in range(3):
            p3_copy(b, r).start()

    def index_keys(k):
        blocks = []
        for h in range(2):
            d, c = pair(k, h)
            blocks.append(kbuf[d, c, :, 640:768])
        return jnp.concatenate(blocks, axis=0)

    def backward(b):
        for r in range(3):
            p3_copy(b, r).wait_recv()
        diff = dbuf[b]
        md = jnp.concatenate(
            [
                jnp.where(logit[b, j * ROWS : (j + 1) * ROWS] > 0, diff, jnp.zeros_like(diff))
                for j in range(16)
            ],
            axis=0,
        )
        both = lax.dot_general(wq[...], md, NN, preferred_element_type=f32)
        dkt = both[0:128] + both[128:256]
        dkp[b, 0] = dkt[:, 0:128]
        dkp[b, 1] = dkt[:, 128:256]
        u[...] += lax.dot_general(md, index_keys(b), NN, preferred_element_type=f32)
        d1_copy(b).start()

    def pump(r):
        remote(
            kbuf.at[r, core], kbuf.at[r, core], ring_send.at[r], ring_recv.at[r], left
        ).wait_recv()
        mate_copy(r, core).start()

        @pl.when(jnp.logical_or(r < 3, jnp.logical_and(r == 3, core == 0)))
        def _():
            left_copy(r).start()

        @pl.when(r < 4)
        def _():
            e = 8 - r
            remote(
                kbuf.at[e, core], kbuf.at[e, core], ring_send.at[8 + e], ring_recv.at[e], right
            ).wait_recv()
            mate_copy(e, core).start()

            @pl.when(jnp.logical_or(r < 3, core == 1))
            def _():
                right_copy(e).start()

    def step(k, _):
        r = (k + 1) // 2
        own_type = k % 2 == 1

        @pl.when(k == 0)
        def _():
            @pl.when(is_own)
            def _():
                mate_copy(0, 1 - core).wait_recv()

        @pl.when(jnp.logical_and(k > 0, jnp.logical_or(k == 7, own_type != is_own)))
        def _():
            mate_copy(r, 1 - core).wait_recv()

            @pl.when(k < 7)
            def _():
                mate_copy(8 - r, 1 - core).wait_recv()

        for h in range(2):
            d, c = pair(k, h)
            block = kbuf[d, c]
            kab[0, h * ROWS : (h + 1) * ROWS] = block[:, 0:640]
            kab[1, h * ROWS : (h + 1) * ROWS] = jnp.concatenate(
                [block[:, 576:640], block[:, 0:576]], axis=1
            )
        part[k, 0] = target_sum(q_ref, kab, lse_b)

        @pl.when(jnp.logical_and(own_type, k < 7))
        def _():
            pump(jnp.where(is_own, r + 1, r))

        @pl.when(k >= 1)
        def _():
            stage1(k - 1)

        def keep(g, x):
            logit[k, g * 1024 : (g + 1) * 1024] = x

        part[k, 1] = score_sum(iq_ref, index_keys(k), w_b, keep)
        p1_copy(k).start()

        @pl.when(k >= 2)
        def _():
            stage2(k - 2)

        @pl.when(jnp.logical_and(k == 6, jnp.logical_not(is_own)))
        def _():
            pump(4)

        return 0

    @pl.when(is_own)
    def _():
        pump(1)

    q_copy.wait()
    lax.fori_loop(0, STEPS, step, 0)
    stage1(STEPS - 1)

    def tail(b, _):
        @pl.when(jnp.logical_or(b == 3, b == 4))
        def _():
            stage2(b + 3)

        backward(b)

        @pl.when(b >= 2)
        def _():
            key_gradient(b - 2)

        return 0

    lax.fori_loop(0, STEPS, tail, 0)
    key_gradient(STEPS - 2)
    sums = []
    for j in range(16):
        uj = u[j * ROWS : (j + 1) * ROWS, :]
        cols = slice(j * ROWS, (j + 1) * ROWS)
        dq_v[:, cols] = uj * w_b[j]
        prod = jnp.transpose(uj * iq_ref[:, cols].astype(f32))
        sums.append(jnp.sum(prod, axis=0, keepdims=True) * INDEX_SCALE)
    dw_ref[...] = jnp.concatenate(sums, axis=0)
    dq_copy.start()
    key_gradient(STEPS - 1)

    @pl.when(is_own)
    def _():
        total = None
        for k in range(STEPS):
            for kind in range(2):
                if k + kind > 0:
                    d2_arrival(kind, k).wait_recv()
                x = rd2[kind, k].astype(f32)
                total = x if total is None else total + x
        fin[xl] = total.astype(bf16)
        for r in range(3):
            fin_copy(r).start()
        fin_copy(1).wait_recv()

    @pl.when(jnp.logical_not(is_own))
    def _():
        fin_copy(0).wait_recv()
        fin_copy(2).wait_recv()

    dk_ref[...] = jnp.transpose(fin[0].astype(f32) + fin[1].astype(f32))
    dq_copy.wait()

    @pl.when(is_own)
    def _():
        for r in range(3):
            fin_copy(r).wait_send()
        cross_copy().wait_send()

    def drain(k, _):
        p1_copy(k).wait_send()
        p2_copy(k).wait_send()
        for r in range(3):
            p3_copy(k, r).wait_send()
        d1_copy(k).wait_send()

        @pl.when(jnp.logical_or(k > 0, jnp.logical_not(is_own)))
        def _():
            d2_copy(k).wait_send()
            mate_copy(k, core).wait_send()

        @pl.when(jnp.logical_or(k < 3, jnp.logical_and(k == 3, core == 0)))
        def _():
            left_copy(k).wait_send()

        @pl.when(jnp.logical_or(k < 3, jnp.logical_and(k == 3, core == 1)))
        def _():
            right_copy((8 - k) % 8).wait_send()

        return 0

    lax.fori_loop(0, STEPS, drain, 0)


def finish(dq_in, dw_in, dk_in, dq_out, dw_out, dk_out):
    dq_out[...] = dq_in[...]
    dw_out[...] = dw_in[...]
    dk_out[...] = dk_in[...]


def body(
    attn_query, key_latent, lse_attn, index_query, index_key, index_weight, lse_index, block_order
):
    sds = jax.ShapeDtypeStruct
    vm = pl.BlockSpec(memory_space=pltpu.VMEM)
    dma = pltpu.SemaphoreType.DMA
    anywhere = pl.BlockSpec(memory_space=pl.ANY)
    outs = (sds((ROWS, 2048), f32), sds((16, ROWS), f32), sds((ROWS, ROWS), f32))
    results = pl.pallas_call(
        kernel,
        out_shape=outs,
        in_specs=[anywhere, vm, vm, anywhere, vm, vm, vm, pl.BlockSpec(memory_space=pltpu.SMEM)],
        out_specs=(anywhere, vm, vm),
        scratch_shapes=[
            pltpu.VMEM((2048, ROWS), f32),
            pltpu.VMEM((ROWS, 2048), f32),
            pltpu.VMEM((ROWS, 2048), bf16),
            pltpu.VMEM((ROWS, 18432), bf16),
            pltpu.VMEM((8, 2, ROWS, 768), bf16),
            pltpu.VMEM((2, PAIR, 640), bf16),
            pltpu.VMEM((32, ROWS, ROWS), f32),
            pltpu.VMEM((16, ROWS, ROWS), f32),
            pltpu.VMEM((ROWS, ROWS), f32),
            pltpu.VMEM((PAIR, 2048), bf16),
            pltpu.VMEM((STEPS, 2048, PAIR), bf16),
            pltpu.VMEM((STEPS, 2, ROWS, PAIR), f32),
            pltpu.VMEM((STEPS, 2, 64, PAIR), f32),
            pltpu.VMEM((STEPS, 2, 32, PAIR), f32),
            pltpu.VMEM((STEPS, 2, 32, PAIR), f32),
            pltpu.VMEM((STEPS, 2, 32, PAIR), f32),
            pltpu.VMEM((STEPS, ROWS, PAIR), bf16),
            pltpu.VMEM((STEPS, 2, ROWS, ROWS), f32),
            pltpu.VMEM((STEPS, ROWS, ROWS), f32),
            pltpu.VMEM((STEPS, ROWS, ROWS), bf16),
            pltpu.VMEM((2, STEPS, ROWS, ROWS), bf16),
            pltpu.VMEM((2, ROWS, ROWS), bf16),
            dma(()),
            dma(()),
            dma(()),
            dma((2,)),
            dma((16,)),
            dma((8,)),
            dma((8,)),
            dma((8,)),
            dma((STEPS,)),
            dma((STEPS,)),
            dma((STEPS,)),
            dma((STEPS,)),
            dma((STEPS, 3)),
            dma((STEPS, 3)),
            dma((STEPS,)),
            dma((STEPS,)),
            dma((STEPS,)),
            dma((2, STEPS)),
            dma((3,)),
            dma((3,)),
        ],
        compiler_params=pltpu.CompilerParams(
            vmem_limit_bytes=56 << 20, collective_id=0, has_side_effects=True
        ),
        name="indexer",
    )(
        attn_query, jnp.transpose(key_latent), lse_attn, index_query, index_key, index_weight,
        lse_index.reshape(1, ROWS), block_order,
    )
    specs = (
        pl.BlockSpec((ROWS, 1024), lambda g: (0, g)),
        pl.BlockSpec((16, ROWS), lambda g: (0, 0)),
        pl.BlockSpec((ROWS, ROWS), lambda g: (0, 0)),
    )
    return pl.pallas_call(
        finish, grid=(2,), out_shape=outs, in_specs=list(specs), out_specs=specs, name="finish"
    )(*results)


def solution(mesh):
    in_specs = (
        P(("seq", "wide"), "narrow"),
        P(("seq", "wide"), None),
        P("narrow", ("seq", "wide")),
        P(("seq", "wide"), "narrow"),
        P(("seq", "wide"), None),
        P("narrow", ("seq", "wide")),
        P(("seq", "wide")),
        P("seq"),
    )
    out_specs = (
        P(("seq", "wide"), "narrow"),
        P("narrow", ("seq", "wide")),
        P(("seq", "wide"), None),
    )
    return jax.shard_map(body, mesh=mesh, in_specs=in_specs, out_specs=out_specs, check_vma=False)
```

```python
import jax
import jax.numpy as jnp
from jax import lax
from jax.experimental import pallas as pl
from jax.experimental.pallas import tpu as pltpu
from jax.sharding import PartitionSpec as P

HEADS = 128
LOG2E = 1.4426950408889634
ATTN_SCALE2 = 192.0 ** (-0.5) * LOG2E
INDEX_SCALE = 128.0 ** (-0.5)
ROWS = 128
FEATURES = 704
HALF = 352
PAIR = 256
STEPS = 8
NT = (((1,), (1,)), ((), ()))
NN = (((1,), (0,)), ((), ()))
f32 = jnp.float32
bf16 = jnp.bfloat16
MESH = pl.DeviceIdType.MESH


def twice(x):
    return jnp.concatenate([x, x], axis=1)


def target_sum(q_ref, kab, lse_b):
    group = 4
    total = None
    for g in range(16 // group):
        for par in range(2):
            parts = [
                q_ref[:, (g * group + i) * 1152 + par * 512 : (g * group + i) * 1152 + par * 512 + 640]
                for i in range(group)
            ]
            s = lax.dot_general(
                jnp.concatenate(parts, axis=0), kab[par], NN, preferred_element_type=f32
            )
            for i in range(group):
                h = (g * group + i) * 2 + par
                e = jnp.exp2(s[i * ROWS : (i + 1) * ROWS] * ATTN_SCALE2 - twice(lse_b[h]))
                total = e if total is None else total + e
    return total


def score_sum(iq_ref, ikey, w_b, keep):
    total = None
    for g in range(2):
        lhs = jnp.concatenate(
            [iq_ref[:, (g * 8 + i) * ROWS : (g * 8 + i + 1) * ROWS] for i in range(8)], axis=0
        )
        s = lax.dot_general(lhs, ikey, NN, preferred_element_type=f32)
        keep(g, s.astype(bf16))
        for i in range(8):
            e = jnp.maximum(s[i * ROWS : (i + 1) * ROWS], 0.0) * twice(w_b[g * 8 + i])
            total = e if total is None else total + e
    return total


def kernel(
    q_hbm, latent_ref, lse_ref, iq_hbm, ikey_ref, weight_ref, lidx_ref, order_ref,
    dq_ref, dw_ref, dk_ref,
    u, dq_v, iq_ref, q_ref, kbuf, kab, lse_b, w_b, lidx_b, wq, logit, part, r1, s2, r2, own2, dbuf, dkp, rd1, sd2, rd2, fin,
    q_sem, iq_sem, dq_sem, cross_sem, ring_send, ring_recv, half_send, half_recv, mate_send, mate_recv,
    p1_send, p1_recv, p2_send, p2_recv, p3_send, p3_recv, d1_send, d1_recv, d2_send, d2_recv,
    fin_send, fin_recv,
):
    wide = lax.axis_index("wide")
    narrow = lax.axis_index("narrow")
    xh, z = wide // 8, wide % 8
    xl, core = narrow // 2, narrow % 2
    is_own = xh == core
    rows64 = pl.multiple_of(core * 64, 64)
    rows32 = pl.multiple_of(core * 64 + xl * 32, 32)
    away32 = pl.multiple_of(core * 64 + (1 - xl) * 32, 32)

    def at(a, b, c, e):
        return {"wide": a * 8 + b, "narrow": c * 2 + e}

    mate = at(xh, z, xl, 1 - core)
    across = at(xh, z, 1 - xl, core)
    others = (mate, across, at(xh, z, 1 - xl, 1 - core))
    right = at(xh, (z + 1) % 8, xl, core)
    left = at(xh, (z + 7) % 8, xl, core)
    cross = at(1 - xh, z, 1 - xl, core)

    def pair(k, h):
        r = (k + 1) // 2
        d = jnp.where(h == 0, r, (8 - r) % 8)
        c = jnp.where((k + 1) % 8 < 2, h, jnp.where(k % 2 == 1, xh, 1 - xh))
        return d, c

    def remote(src, dst, send, recv, dev):
        return pltpu.make_async_remote_copy(
            src_ref=src, dst_ref=dst, send_sem=send, recv_sem=recv, device_id=dev, device_id_type=MESH
        )

    def cross_copy():
        return remote(kbuf.at[0, core], kbuf.at[0, core], cross_sem.at[0], cross_sem.at[1], cross)

    def rows_of(d, own):
        return kbuf.at[d, core] if own else kbuf.at[d, core, pl.ds(0, HALF)]

    def left_copy(d, own):
        return remote(rows_of(d, own), rows_of(d + 1, own), ring_send.at[d], ring_recv.at[d + 1], left)

    def right_copy(d, own):
        e = (d + 7) % 8
        return remote(rows_of(d, own), rows_of(e, own), ring_send.at[8 + d], ring_recv.at[e], right)

    def ring_arrival(d, own):
        return remote(rows_of(d, own), rows_of(d, own), ring_send.at[d], ring_recv.at[d], left)

    def across_half(d):
        half = kbuf.at[d, core, pl.ds(HALF, HALF)]
        return remote(half, half, half_send.at[d], half_recv.at[d], cross)

    def mate_copy(d, c):
        return remote(kbuf.at[d, c], kbuf.at[d, c], mate_send.at[d], mate_recv.at[d], mate)

    def p1_copy(k):
        src = part.at[k, :, pl.ds(pl.multiple_of((1 - core) * 64, 64), 64), :]
        return remote(src, r1.at[k], p1_send.at[k], p1_recv.at[k], mate)

    def p2_copy(k):
        return remote(s2.at[k], r2.at[k], p2_send.at[k], p2_recv.at[k], across)

    def p3_copy(k, r):
        block = dbuf.at[k, pl.ds(rows32, 32), :]
        return remote(block, block, p3_send.at[k, r], p3_recv.at[k, r], others[r])

    def d1_copy(k):
        return remote(dkp.at[k, 1 - core], rd1.at[k], d1_send.at[k], d1_recv.at[k], mate)

    def d2_copy(k):
        d, c = pair(k, core)
        kind = jnp.where(c == xh, 0, 1)
        dev = at(c, (z + d) % 8, jnp.where(c == xh, xl, 1 - xl), c)
        return remote(sd2.at[k], rd2.at[kind, d], d2_send.at[k], d2_recv.at[kind, d], dev)

    def d2_arrival(kind, d):
        return remote(sd2.at[d], rd2.at[kind, d], d2_send.at[d], d2_recv.at[kind, d], mate)

    def fin_copy(r):
        return remote(fin.at[xl], fin.at[xl], fin_send.at[r], fin_recv.at[r], others[r])

    q_copy = pltpu.make_async_copy(q_hbm, q_ref, q_sem)
    iq_copy = pltpu.make_async_copy(iq_hbm, iq_ref, iq_sem)
    dq_copy = pltpu.make_async_copy(dq_v, dq_ref, dq_sem)
    barrier = pltpu.get_barrier_semaphore()
    for dev in others + (right, left, cross):
        pl.semaphore_signal(barrier, inc=1, device_id=dev, device_id_type=MESH)
    iq_copy.start()
    q_copy.start()
    kbuf[0, xh, 0:576, :] = latent_ref[...]
    kbuf[0, xh, 576:704, :] = jnp.transpose(ikey_ref[...].astype(f32)).astype(bf16)
    pl.semaphore_wait(barrier, 6)

    @pl.when(is_own)
    def _():
        cross_copy().start()
        left_copy(0, True).start()
        right_copy(0, True).start()

    lse_t = jnp.transpose(lse_ref[...]) * LOG2E
    for h in range(32):
        lse_b[h] = jnp.broadcast_to(lse_t[:, h : h + 1], (ROWS, ROWS))
    w_t = jnp.transpose(weight_ref[...]) * INDEX_SCALE
    for j in range(16):
        w_b[j] = jnp.broadcast_to(w_t[:, j : j + 1], (ROWS, ROWS))
    kab[0, 576:640, :] = jnp.zeros((64, PAIR), bf16)
    kab[1, 0:64, :] = jnp.zeros((64, PAIR), bf16)
    lidx_b[...] = jnp.transpose(jnp.broadcast_to(lidx_ref[...], (ROWS, ROWS)))

    @pl.when(jnp.logical_not(is_own))
    def _():
        cross_copy().wait_recv()
        mate_copy(0, core).start()
        left_copy(0, False).start()
        right_copy(0, False).start()

    iq_copy.wait()
    for j in range(16):
        x = jnp.transpose(iq_ref[:, j * ROWS : (j + 1) * ROWS].astype(f32))
        x = x * (weight_ref[j : j + 1, :] * INDEX_SCALE)
        hi = x.astype(bf16)
        wq[0:128, j * ROWS : (j + 1) * ROWS] = hi
        wq[128:256, j * ROWS : (j + 1) * ROWS] = (x - hi.astype(f32)).astype(bf16)
    u[...] = jnp.zeros_like(u)

    def key_gradient(k):
        d1_copy(k).wait_recv()
        total = (dkp[k, core] + rd1[k]).astype(bf16)
        here = jnp.logical_and(k == 0, is_own)

        @pl.when(here)
        def _():
            rd2[0, 0] = total

        @pl.when(jnp.logical_not(here))
        def _():
            sd2[k] = total
            d2_copy(k).start()

    def stage1(b):
        p1_copy(b).wait_recv()
        far = pl.multiple_of((1 - xl) * 32, 32)
        near = pl.multiple_of(xl * 32, 32)
        for a in range(2):
            s2[b, a] = part[b, a, pl.ds(away32, 32), :] + r1[b, a, pl.ds(far, 32), :]
        p2_copy(b).start()
        for a in range(2):
            own2[b, a] = part[b, a, pl.ds(rows32, 32), :] + r1[b, a, pl.ds(near, 32), :]

    def stage2(b):
        p2_copy(b).wait_recv()
        target = own2[b, 0] + r2[b, 0]
        score = own2[b, 1] + r2[b, 1]
        lidx = lidx_b[pl.ds(rows32, 32), :]
        row = order_ref[wide] * ROWS + rows32 + lax.broadcasted_iota(jnp.int32, (32, ROWS), 0)
        lane = lax.broadcasted_iota(jnp.int32, (32, ROWS), 1)
        causal = []
        for h in range(2):
            d, c = pair(b, h)
            causal.append(row >= order_ref[c * 8 + (z + d) % 8] * ROWS + lane)
        diff = jnp.exp(score - twice(lidx)) - target * (1.0 / HEADS)
        diff = jnp.where(jnp.concatenate(causal, axis=1), diff, 0.0)
        dbuf[b, pl.ds(rows32, 32), :] = diff.astype(bf16)
        for r in range(3):
            p3_copy(b, r).start()

    def index_keys(k):
        blocks = []
        for h in range(2):
            d, c = pair(k, h)
            blocks.append(kbuf[d, c, 576:704, :])
        return jnp.concatenate(blocks, axis=1)

    def backward(b):
        for r in range(3):
            p3_copy(b, r).wait_recv()
        diff = dbuf[b]
        md = jnp.concatenate(
            [
                jnp.where(logit[b, j * ROWS : (j + 1) * ROWS] > 0, diff, jnp.zeros_like(diff))
                for j in range(16)
            ],
            axis=0,
        )
        both = lax.dot_general(wq[...], md, NN, preferred_element_type=f32)
        dkt = both[0:128] + both[128:256]
        dkp[b, 0] = dkt[:, 0:128]
        dkp[b, 1] = dkt[:, 128:256]
        u[...] += lax.dot_general(md, index_keys(b), NT, preferred_element_type=f32)
        d1_copy(b).start()

    def share(d, own):
        if own:
            across_half(d).start()
        else:
            across_half(d).wait_recv()
        mate_copy(d, core).start()

    def pump(r, own):
        ring_arrival(r, own).wait_recv()

        @pl.when(jnp.logical_or(r < 3, jnp.logical_and(r == 3, core == 0)))
        def _():
            left_copy(r, own).start()

        share(r, own)

        @pl.when(r < 4)
        def _():
            e = 8 - r
            ring_arrival(e, own).wait_recv()

            @pl.when(jnp.logical_or(r < 3, core == 1))
            def _():
                right_copy(e, own).start()

            share(e, own)

    def step(k, _):
        r = (k + 1) // 2
        own_type = k % 2 == 1

        @pl.when(k == 0)
        def _():
            @pl.when(is_own)
            def _():
                mate_copy(0, 1 - core).wait_recv()

        @pl.when(jnp.logical_and(k > 0, jnp.logical_or(k == 7, own_type != is_own)))
        def _():
            mate_copy(r, 1 - core).wait_recv()

            @pl.when(k < 7)
            def _():
                mate_copy(8 - r, 1 - core).wait_recv()

        for h in range(2):
            d, c = pair(k, h)
            latent = kbuf[d, c, 0:576, :]
            kab[0, 0:576, h * ROWS : (h + 1) * ROWS] = latent
            kab[1, 64:640, h * ROWS : (h + 1) * ROWS] = latent
        part[k, 0] = target_sum(q_ref, kab, lse_b)

        @pl.when(jnp.logical_and(own_type, k < 7))
        def _():
            @pl.when(is_own)
            def _():
                pump(r + 1, True)

            @pl.when(jnp.logical_not(is_own))
            def _():
                pump(r, False)

        @pl.when(k >= 1)
        def _():
            stage1(k - 1)

        def keep(g, x):
            logit[k, g * 1024 : (g + 1) * 1024] = x

        part[k, 1] = score_sum(iq_ref, index_keys(k), w_b, keep)
        p1_copy(k).start()

        @pl.when(k >= 2)
        def _():
            stage2(k - 2)

        @pl.when(jnp.logical_and(k == 6, jnp.logical_not(is_own)))
        def _():
            pump(4, False)

        return 0

    @pl.when(is_own)
    def _():
        pump(1, True)

    q_copy.wait()
    lax.fori_loop(0, STEPS, step, 0)
    stage1(STEPS - 1)

    def tail(b, _):
        @pl.when(jnp.logical_or(b == 3, b == 4))
        def _():
            stage2(b + 3)

        backward(b)

        @pl.when(b >= 2)
        def _():
            key_gradient(b - 2)

        return 0

    lax.fori_loop(0, STEPS, tail, 0)
    key_gradient(STEPS - 2)
    sums = []
    for j in range(16):
        uj = u[j * ROWS : (j + 1) * ROWS, :]
        cols = slice(j * ROWS, (j + 1) * ROWS)
        dq_v[:, cols] = uj * w_b[j]
        prod = jnp.transpose(uj * iq_ref[:, cols].astype(f32))
        sums.append(jnp.sum(prod, axis=0, keepdims=True) * INDEX_SCALE)
    dw_ref[...] = jnp.concatenate(sums, axis=0)
    dq_copy.start()
    key_gradient(STEPS - 1)

    @pl.when(is_own)
    def _():
        total = None
        for k in range(STEPS):
            for kind in range(2):
                if k + kind > 0:
                    d2_arrival(kind, k).wait_recv()
                x = rd2[kind, k].astype(f32)
                total = x if total is None else total + x
        fin[xl] = total.astype(bf16)
        for r in range(3):
            fin_copy(r).start()
        fin_copy(1).wait_recv()

    @pl.when(jnp.logical_not(is_own))
    def _():
        fin_copy(0).wait_recv()
        fin_copy(2).wait_recv()

    dk_ref[...] = jnp.transpose(fin[0].astype(f32) + fin[1].astype(f32))
    dq_copy.wait()

    @pl.when(is_own)
    def _():
        for r in range(3):
            fin_copy(r).wait_send()
        cross_copy().wait_send()

    def drain(k, _):
        p1_copy(k).wait_send()
        p2_copy(k).wait_send()
        for r in range(3):
            p3_copy(k, r).wait_send()
        d1_copy(k).wait_send()

        @pl.when(jnp.logical_or(k > 0, jnp.logical_not(is_own)))
        def _():
            d2_copy(k).wait_send()
            mate_copy(k, core).wait_send()

        def sent(own):
            @pl.when(jnp.logical_or(k < 3, jnp.logical_and(k == 3, core == 0)))
            def _():
                left_copy(k, own).wait_send()

            @pl.when(jnp.logical_or(k < 3, jnp.logical_and(k == 3, core == 1)))
            def _():
                right_copy((8 - k) % 8, own).wait_send()

        @pl.when(is_own)
        def _():
            sent(True)

            @pl.when(k > 0)
            def _():
                across_half(k).wait_send()

        @pl.when(jnp.logical_not(is_own))
        def _():
            sent(False)

        return 0

    lax.fori_loop(0, STEPS, drain, 0)


def finish(dq_in, dw_in, dk_in, dq_out, dw_out, dk_out):
    dq_out[...] = dq_in[...]
    dw_out[...] = dw_in[...]
    dk_out[...] = dk_in[...]


def body(
    attn_query, key_latent, lse_attn, index_query, index_key, index_weight, lse_index, block_order
):
    sds = jax.ShapeDtypeStruct
    vm = pl.BlockSpec(memory_space=pltpu.VMEM)
    dma = pltpu.SemaphoreType.DMA
    anywhere = pl.BlockSpec(memory_space=pl.ANY)
    outs = (sds((ROWS, 2048), f32), sds((16, ROWS), f32), sds((ROWS, ROWS), f32))
    results = pl.pallas_call(
        kernel,
        out_shape=outs,
        in_specs=[anywhere, vm, vm, anywhere, vm, vm, vm, pl.BlockSpec(memory_space=pltpu.SMEM)],
        out_specs=(anywhere, vm, vm),
        scratch_shapes=[
            pltpu.VMEM((2048, ROWS), f32),
            pltpu.VMEM((ROWS, 2048), f32),
            pltpu.VMEM((ROWS, 2048), bf16),
            pltpu.VMEM((ROWS, 18432), bf16),
            pltpu.VMEM((8, 2, FEATURES, ROWS), bf16),
            pltpu.VMEM((2, 640, PAIR), bf16),
            pltpu.VMEM((32, ROWS, ROWS), f32),
            pltpu.VMEM((16, ROWS, ROWS), f32),
            pltpu.VMEM((ROWS, ROWS), f32),
            pltpu.VMEM((PAIR, 2048), bf16),
            pltpu.VMEM((STEPS, 2048, PAIR), bf16),
            pltpu.VMEM((STEPS, 2, ROWS, PAIR), f32),
            pltpu.VMEM((STEPS, 2, 64, PAIR), f32),
            pltpu.VMEM((STEPS, 2, 32, PAIR), f32),
            pltpu.VMEM((STEPS, 2, 32, PAIR), f32),
            pltpu.VMEM((STEPS, 2, 32, PAIR), f32),
            pltpu.VMEM((STEPS, ROWS, PAIR), bf16),
            pltpu.VMEM((STEPS, 2, ROWS, ROWS), f32),
            pltpu.VMEM((STEPS, ROWS, ROWS), f32),
            pltpu.VMEM((STEPS, ROWS, ROWS), bf16),
            pltpu.VMEM((2, STEPS, ROWS, ROWS), bf16),
            pltpu.VMEM((2, ROWS, ROWS), bf16),
            dma(()),
            dma(()),
            dma(()),
            dma((2,)),
            dma((16,)),
            dma((8,)),
            dma((8,)),
            dma((8,)),
            dma((8,)),
            dma((8,)),
            dma((STEPS,)),
            dma((STEPS,)),
            dma((STEPS,)),
            dma((STEPS,)),
            dma((STEPS, 3)),
            dma((STEPS, 3)),
            dma((STEPS,)),
            dma((STEPS,)),
            dma((STEPS,)),
            dma((2, STEPS)),
            dma((3,)),
            dma((3,)),
        ],
        compiler_params=pltpu.CompilerParams(
            vmem_limit_bytes=56 << 20, collective_id=0, has_side_effects=True
        ),
        name="indexer",
    )(
        attn_query, jnp.transpose(key_latent), lse_attn, index_query, index_key, index_weight,
        lse_index.reshape(1, ROWS), block_order,
    )
    specs = (
        pl.BlockSpec((ROWS, 1024), lambda g: (0, g)),
        pl.BlockSpec((16, ROWS), lambda g: (0, 0)),
        pl.BlockSpec((ROWS, ROWS), lambda g: (0, 0)),
    )
    return pl.pallas_call(
        finish, grid=(2,), out_shape=outs, in_specs=list(specs), out_specs=specs, name="finish"
    )(*results)


def solution(mesh):
    in_specs = (
        P(("seq", "wide"), "narrow"),
        P(("seq", "wide"), None),
        P("narrow", ("seq", "wide")),
        P(("seq", "wide"), "narrow"),
        P(("seq", "wide"), None),
        P("narrow", ("seq", "wide")),
        P(("seq", "wide")),
        P("seq"),
    )
    out_specs = (
        P(("seq", "wide"), "narrow"),
        P("narrow", ("seq", "wide")),
        P(("seq", "wide"), None),
    )
    return jax.shard_map(body, mesh=mesh, in_specs=in_specs, out_specs=out_specs, check_vma=False)
```
